128 devices in a mesh: rows: 128 (over y, z, x, core).
Axes of the slice: x: 4, y: 4, z: 4, core: 2. Of those that a mesh axis runs over, the one named last changes fastest.
Arguments:
- slab: bfloat16 [262144, 4096], P('rows'), may hold values from -60 to 60, as said below
- test_matrix: bfloat16 [4096, 128], replicated, may hold values from -0.09375 to 0.09375
Outputs:
- projected: float32 [128, 4096], P(None, 'rows')
The draws below stay inside these ranges and needn't reach their ends.
Inputs may be any that keep to these rules, and one draw needn't show every extreme that they name: Entries of the slab are of order one to some tens.
All inputs are finite; a program needn't handle non-finite values.
Results may differ from the reference program's by a relative error of at most 0.0003.
Values sent between devices are 32-bit elements; how exact they have to be, the bound alone decides.
No kernel may reach another device: no remote copies, remote signals or barrier semaphores. Data moves between devices by JAX's collectives and lax.ppermute only.
A program may use at most 64 MiB of HBM per device.

```python
import math
import jax
import jax.numpy as jnp
from jax import lax

D = 4096
K = 128
ROWS = 262144


def draw_slab(key, part):
    key = jax.random.fold_in(key, 1)
    keys = jax.random.split(key, 3)
    position = jnp.arange(ROWS).astype(jnp.float32)
    rising = 1.0 + 2.0 * position / (ROWS - 1)
    row_scale = jnp.exp(jax.random.uniform(keys[1], (ROWS, 1), jnp.float32) * math.log(10.0)) * rising[:, None]
    col_scale = jnp.exp(jax.random.uniform(keys[2], (1, D), jnp.float32) * math.log(10.0))
    values = jnp.clip(jax.random.normal(keys[0], (ROWS, D), jnp.float32), -6.0, 6.0)
    return (values * row_scale * col_scale / 30.0).astype(jnp.bfloat16)


def bell_draw(stream_key, extent, scale, bound, kind=jnp.bfloat16):
    array = jax.random.normal(stream_key, extent, jnp.float32) * scale
    return jnp.minimum(jnp.maximum(array, -bound), bound).astype(kind)


def setup_inputs(seed: int = 0) -> dict:
    key_of = jax.random.split(jax.random.key(seed), 3)
    slab = draw_slab(jax.random.fold_in(key_of[2], 71), 0)
    test_matrix = bell_draw(key_of[1], (D, K), D ** -0.5, 0.09375)
    return dict(slab=slab, test_matrix=test_matrix)


highest = lax.Precision.HIGHEST

def cholesky_lower(gram_sum):
    order = gram_sum.shape[0]
    places = jnp.arange(order, dtype=jnp.int32)

    def column_step(index, lower):
        unit = (places == index).astype(jnp.float32)
        column = jnp.dot(gram_sum, unit, precision=highest)
        row_of_l = jnp.dot(unit, lower, precision=highest)
        column = column - jnp.dot(lower, row_of_l, precision=highest)
        pivot = jnp.sqrt(jnp.dot(unit, column, precision=highest))
        keep = (places >= index).astype(jnp.float32)
        return lower + jnp.outer(column * keep / pivot, unit)
    return lax.fori_loop(0, order, column_step, jnp.zeros((order, order), jnp.float32))

def invert_lower(lower):
    order = lower.shape[0]
    places = jnp.arange(order, dtype=jnp.int32)

    def row_step(index, inverse):
        unit = (places == index).astype(jnp.float32)
        row_of_l = jnp.dot(unit, lower, precision=highest)
        pivot = jnp.dot(row_of_l, unit, precision=highest)
        below = row_of_l * (places < index).astype(jnp.float32)
        new_row = (unit - jnp.dot(below, inverse, precision=highest)) / pivot
        return inverse + jnp.outer(unit, new_row)
    return lax.fori_loop(0, order, row_step, jnp.zeros((order, order), jnp.float32))

def reference(slab, test_matrix):
    sketch = jnp.dot(slab, test_matrix, preferred_element_type=jnp.float32)
    gram_sum = jnp.dot(sketch.T, sketch, precision=highest)
    inverse_l = invert_lower(cholesky_lower(gram_sum))
    basis_q = jnp.dot(sketch, inverse_l.T, precision=highest)
    block_rows = min(8192, ROWS)
    block_count = ROWS // block_rows
    basis_blocks = basis_q.reshape(block_count, block_rows, K)
    slab_blocks = slab.reshape(block_count, block_rows, D)

    def advance(running, entry):
        left_part, slab_part = entry
        return (running + jnp.dot(left_part.T, slab_part.astype(basis_q.dtype), precision=highest), None)
    start = jnp.zeros((K, D), basis_q.dtype)
    projected, _ = lax.scan(advance, start, (basis_blocks, slab_blocks))
    return projected
```

```python
import functools

import jax
import jax.numpy as jnp
from jax import lax
from jax.experimental import pallas as pl
from jax.experimental.pallas import tpu as pltpu
from jax.sharding import Mesh, PartitionSpec as P

AXES = ("y", "z", "x", "c")
CHIPS = ("y", "z", "x")
K = 128
CHUNK = 256
COLS = 256
NT = (((1,), (1,)), ((), ()))


def sketch_kernel(place_ref, slab_ref, omega_t_ref, gram_ref, mine_ref, other_ref, slab_v, parts, sems):
    rows, width = slab_v.shape
    chunks = rows // CHUNK

    def copy(i):
        at = pl.ds(i * CHUNK, CHUNK)
        return pltpu.make_async_copy(slab_ref.at[at, :], slab_v.at[at, :], sems.at[i])

    for i in range(chunks):
        copy(i).start()
    for i in range(chunks):
        copy(i).wait()
        block = slab_v[pl.ds(i * CHUNK, CHUNK), :]
        sketch_t = lax.dot_general(omega_t_ref[...], block, NT, preferred_element_type=jnp.float32)
        high = sketch_t.astype(jnp.bfloat16)
        low = (sketch_t - high.astype(jnp.float32)).astype(jnp.bfloat16)
        parts[pl.ds(0, K), pl.ds(i * CHUNK, CHUNK)] = high
        parts[pl.ds(K, K), pl.ds(i * CHUNK, CHUNK)] = low
    quad = lax.dot_general(parts[...], parts[...], NT, preferred_element_type=jnp.float32)
    gram_ref[...] = (quad[K:, K:] + (quad[:K, K:] + quad[K:, :K])) + quad[:K, :K]

    core = place_ref[0]
    per_tile = COLS // 64

    def column_tile(n, carry):
        both = jnp.dot(
            parts[...], slab_v[:, pl.ds(pl.multiple_of(n * COLS, COLS), COLS)],
            preferred_element_type=jnp.float32,
        )
        tile = (both[K:, :] + both[:K, :]).T.reshape(per_tile, 2, 32, K)
        at = pl.ds(n * per_tile, per_tile)

        @pl.when(core == 0)
        def _():
            mine_ref[at] = tile[:, 0]
            other_ref[at] = tile[:, 1]

        @pl.when(core == 1)
        def _():
            mine_ref[at] = tile[:, 1]
            other_ref[at] = tile[:, 0]

        return carry

    lax.fori_loop(0, width // COLS, column_tile, 0)


def sketch_call(place, slab, omega_t):
    rows, width = slab.shape
    chips = width // 64
    vmem = pl.BlockSpec(memory_space=pltpu.VMEM)
    half = jax.ShapeDtypeStruct((chips, 32, K), jnp.float32)
    return pl.pallas_call(
        sketch_kernel,
        out_shape=(jax.ShapeDtypeStruct((K, K), jnp.float32), half, half),
        in_specs=[
            pl.BlockSpec(memory_space=pltpu.SMEM),
            pl.BlockSpec(memory_space=pl.ANY),
            vmem,
        ],
        out_specs=(vmem, vmem, vmem),
        scratch_shapes=[
            pltpu.VMEM((rows, width), slab.dtype),
            pltpu.VMEM((2 * K, rows), jnp.bfloat16),
            pltpu.SemaphoreType.DMA((rows // CHUNK,)),
        ],
        compiler_params=pltpu.CompilerParams(vmem_limit_bytes=40 * 2**20),
        cost_estimate=pl.CostEstimate(
            flops=2 * rows * width * 3 * K, bytes_accessed=2 * rows * width, transcendentals=0
        ),
        name="sketch",
    )(place, slab, omega_t)


def reciprocal(value):
    guess = pl.reciprocal(value, approx=True)
    guess = guess * (2.0 - value * guess)
    return guess * (2.0 - value * guess)


def factor_rows(blocks):
    shape = (8, K)
    lane = lax.broadcasted_iota(jnp.int32, shape, 1)
    sublane = lax.broadcasted_iota(jnp.int32, shape, 0)
    blocks = list(blocks)
    count = len(blocks)
    done = []
    for b in range(count):
        first = 8 * b
        inside = (lane >= first) & (lane < first + 8)
        here = blocks[b]
        columns = [jnp.broadcast_to(here[:, first + k : first + k + 1], shape) for k in range(8)]
        entry = {
            (i, k): jnp.broadcast_to(columns[k][i : i + 1, :], shape) for k in range(8) for i in range(k, 8)
        }
        cleared = jnp.where(inside, (lane - first == sublane).astype(jnp.float32), here)
        rows = [jnp.broadcast_to(cleared[k : k + 1, :], shape) for k in range(8)]
        inverse_pivot = []
        lower = {}
        for k in range(8):
            inverse = reciprocal(entry[k, k])
            inverse_pivot.append(inverse)
            for i in range(k + 1, 8):
                lower[i, k] = entry[i, k] * inverse
            for i in range(k + 1, 8):
                for j in range(k + 1, i + 1):
                    entry[i, j] = entry[i, j] - (entry[i, k] * entry[j, k]) * inverse
        for k in range(8):
            for m in range(k):
                rows[k] = rows[k] - lower[k, m] * rows[m]
        result = jnp.zeros(shape, jnp.float32)
        for k in range(8):
            result = jnp.where(sublane == k, rows[k] * lax.rsqrt(entry[k, k]), result)
        done.append(jnp.where(lane <= first + sublane, result, 0.0))
        for i in range(b + 1, count):
            target = blocks[i]
            factors = [jnp.broadcast_to(target[:, first + k : first + k + 1], shape) for k in range(8)]
            target = jnp.where(inside, 0.0, target)
            for k in range(8):
                factor = factors[k]
                for m in range(k):
                    factor = factor - factors[m] * entry[k, m]
                factor = factor * inverse_pivot[k]
                factors[k] = factor
                target = target - factor * rows[k]
            blocks[i] = target
    return done


def factor_kernel(gram_ref, inverse_ref):
    blocks = [gram_ref[pl.ds(8 * b, 8), :] for b in range(K // 8)]
    for b, rows in enumerate(factor_rows(blocks)):
        inverse_ref[pl.ds(8 * b, 8), :] = rows


def factor_call(gram):
    vmem = pl.BlockSpec(memory_space=pltpu.VMEM)
    return pl.pallas_call(
        factor_kernel,
        out_shape=jax.ShapeDtypeStruct((K, K), jnp.float32),
        in_specs=[vmem],
        out_specs=vmem,
        cost_estimate=pl.CostEstimate(flops=10**9, bytes_accessed=2**17, transcendentals=0),
        name="factor",
    )(gram)


def project_kernel(inverse_ref, pieces_ref, out_ref):
    total = jnp.sum(pieces_ref[...], axis=0)
    out_ref[...] = lax.dot_general(
        inverse_ref[...], total, NT, precision=lax.Precision.HIGHEST, preferred_element_type=jnp.float32
    )


def project_call(inverse, pieces):
    vmem = pl.BlockSpec(memory_space=pltpu.VMEM)
    return pl.pallas_call(
        project_kernel,
        out_shape=jax.ShapeDtypeStruct((K, pieces.shape[1]), jnp.float32),
        in_specs=[vmem, vmem],
        out_specs=vmem,
        name="project",
    )(inverse, pieces)


def shift(array, axis, size, by):
    return lax.ppermute(array, axis, [(i, (i + by) % size) for i in range(size)])


def sum_over_rows(gram):
    gram = gram + shift(gram, "c", 2, 1)
    for axis in ("x", "z", "y"):
        gram = (gram + shift(gram, axis, 4, 2)) + (shift(gram, axis, 4, 1) + shift(gram, axis, 4, -1))
    return gram


def body(slab, test_matrix):
    place = lax.axis_index("c").astype(jnp.int32).reshape(1)
    gram, mine, other = sketch_call(place, slab, test_matrix.T)
    half = mine + shift(other, "c", 2, 1)
    pieces = lax.all_to_all(half, CHIPS, 0, 0, tiled=True)
    inverse = factor_call(sum_over_rows(gram))
    return project_call(inverse, pieces)


def solution(mesh):
    grid = Mesh(mesh.devices.reshape(4, 4, 4, 2), AXES)
    return jax.shard_map(
        body, mesh=grid, in_specs=(P(AXES, None), P()), out_specs=P(None, AXES), check_vma=False
    )
```

```python
import jax
import jax.numpy as jnp
from jax import lax
from jax.experimental import pallas as pl
from jax.experimental.pallas import tpu as pltpu
from jax.sharding import Mesh, PartitionSpec as P

AXES = ("y", "z", "x", "c")
K = 128
CHUNK = 256
AHEAD = 3
COLS = 512
NT = (((1,), (1,)), ((), ()))


def sketch_kernel(place_ref, slab_ref, omega_ref, gram_ref, mine_ref, other_ref, slab_v, omega_v, beside, above, sems, omega_sem):
    rows, width = slab_v.shape
    chunks = rows // CHUNK

    def copy(i):
        at = pl.ds(i * CHUNK, CHUNK)
        return pltpu.make_async_copy(slab_ref.at[at, :], slab_v.at[at, :], sems.at[i])

    def split(value):
        high = value.astype(jnp.bfloat16)
        return high, (value - high.astype(jnp.float32)).astype(jnp.bfloat16)

    omega_copy = pltpu.make_async_copy(omega_ref, omega_v, omega_sem)
    omega_copy.start()
    copy(0).start()
    omega_copy.wait()
    for i in range(1, AHEAD):
        copy(i).start()
    for i in range(chunks):
        copy(i).wait()
        if i + AHEAD < chunks:
            copy(i + AHEAD).start()
        at = pl.ds(i * CHUNK, CHUNK)
        sketch = jnp.dot(slab_v[at, :], omega_v[...], preferred_element_type=jnp.float32)
        beside[at, :K], beside[at, K:] = split(sketch)
        above[:K, at], above[K:, at] = split(sketch.T)
    gram = jnp.dot(above[...], beside[...], preferred_element_type=jnp.float32)
    gram_ref[...] = (gram[K:, K:] + (gram[:K, K:] + gram[K:, :K])) + gram[:K, :K]

    core = place_ref[0]
    groups = COLS // 256
    for n in range(width // COLS):
        both = jnp.dot(above[...], slab_v[:, pl.ds(n * COLS, COLS)], preferred_element_type=jnp.float32)
        tile = (both[K:, :] + both[:K, :]).T.reshape(groups, 4, 2, 32, K)
        at = pl.ds(n * groups, groups)
        for x in range(4):
            even, odd = tile[:, x, 0], tile[:, x, 1]
            mine_ref[x, at] = jnp.where(core == 0, even, odd)
            other_ref[x, at] = jnp.where(core == 0, odd, even)


def sketch_call(place, slab, omega):
    rows, width = slab.shape
    vmem = pl.BlockSpec(memory_space=pltpu.VMEM)
    hbm = pl.BlockSpec(memory_space=pltpu.HBM)
    half = jax.ShapeDtypeStruct((4, width // 256, 32, K), jnp.float32)
    return pl.pallas_call(
        sketch_kernel,
        out_shape=(jax.ShapeDtypeStruct((K, K), jnp.float32), half, half),
        in_specs=[pl.BlockSpec(memory_space=pltpu.SMEM), hbm, hbm],
        out_specs=(vmem,) * 3,
        scratch_shapes=[
            pltpu.VMEM((rows, width), slab.dtype),
            pltpu.VMEM(omega.shape, omega.dtype),
            pltpu.VMEM((rows, 2 * K), jnp.bfloat16),
            pltpu.VMEM((2 * K, rows), jnp.bfloat16),
            pltpu.SemaphoreType.DMA((rows // CHUNK,)),
            pltpu.SemaphoreType.DMA,
        ],
        compiler_params=pltpu.CompilerParams(vmem_limit_bytes=36 * 2**20),
        cost_estimate=pl.CostEstimate(
            flops=2 * rows * width * 3 * K, bytes_accessed=2 * rows * width, transcendentals=0
        ),
        name="sketch",
    )(place, slab, omega)


def factor_rows(blocks):
    shape = (8, K)
    lane = lax.broadcasted_iota(jnp.int32, shape, 1)
    sublane = lax.broadcasted_iota(jnp.int32, shape, 0)
    blocks = list(blocks)
    count = len(blocks)
    done = []

    def column(array, at):
        return jnp.broadcast_to(array[:, at : at + 1], shape)

    def row(array, at):
        return jnp.broadcast_to(array[at : at + 1, :], shape)

    for b in range(count):
        first = 8 * b
        inside = (lane >= first) & (lane < first + 8)
        columns = [column(blocks[b], first + k) for k in range(8)]
        entry = {(i, k): row(columns[k], i) for k in range(8) for i in range(k, 8)}
        cleared = jnp.where(inside, (lane - first == sublane).astype(jnp.float32), blocks[b])
        rows = [row(cleared, k) for k in range(8)]
        inverse = [None] * 8
        lower = {}
        for k in range(8):
            inverse[k] = pltpu.reciprocal(entry[k, k], approx=True)
            for i in range(k + 1, 8):
                lower[i, k] = entry[i, k] * inverse[k]
            for i in range(k + 1, 8):
                for j in range(k + 1, i + 1):
                    entry[i, j] = entry[i, j] - lower[i, k] * entry[j, k]
        for k in range(8):
            for m in range(k):
                rows[k] = rows[k] - lower[k, m] * rows[m]
        result = jnp.zeros(shape, jnp.float32)
        for k in range(8):
            result = jnp.where(sublane == k, rows[k] * lax.rsqrt(entry[k, k]), result)
        done.append(jnp.where(lane <= first + sublane, result, 0.0))
        if b + 1 == count:
            break
        target = blocks[b + 1]
        factors = [column(target, first + k) for k in range(8)]
        target = jnp.where(inside, 0.0, target)
        for k in range(8):
            factor = factors[k] * inverse[k]
            for m in range(k + 1, 8):
                factors[m] = factors[m] - factor * entry[m, k]
            target = target - factor * rows[k]
        blocks[b + 1] = target
        solved = [None] * 8
        for k in reversed(range(8)):
            value = rows[k] * inverse[k]
            for m in range(k + 1, 8):
                value = value - lower[m, k] * solved[m]
            solved[k] = value
        for i in range(b + 2, count):
            products = [column(blocks[i], first + k) * solved[k] for k in range(8)]
            while len(products) > 1:
                products = [products[p] + products[p + 1] for p in range(0, len(products), 2)]
            blocks[i] = jnp.where(inside, 0.0, blocks[i]) - products[0]
    return done


def factor_kernel(gram_ref, inverse_ref):
    blocks = [gram_ref[pl.ds(8 * b, 8), :] for b in range(K // 8)]
    for b, rows in enumerate(factor_rows(blocks)):
        inverse_ref[pl.ds(8 * b, 8), :] = rows


def factor_call(gram):
    vmem = pl.BlockSpec(memory_space=pltpu.VMEM)
    return pl.pallas_call(
        factor_kernel,
        out_shape=jax.ShapeDtypeStruct((K, K), jnp.float32),
        in_specs=[vmem],
        out_specs=vmem,
        compiler_params=pltpu.CompilerParams(vmem_limit_bytes=8 * 2**20),
        cost_estimate=pl.CostEstimate(flops=10**9, bytes_accessed=2**17, transcendentals=0),
        name="factor",
    )(gram)


def project_kernel(inverse_ref, pieces_ref, out_ref):
    total = jnp.sum(pieces_ref[...], axis=0)
    out_ref[...] = lax.dot_general(
        total, inverse_ref[...], NT, precision=lax.Precision.HIGHEST, preferred_element_type=jnp.float32
    )


def project_call(inverse, pieces):
    vmem = pl.BlockSpec(memory_space=pltpu.VMEM)
    return pl.pallas_call(
        project_kernel,
        out_shape=jax.ShapeDtypeStruct((pieces.shape[1], K), jnp.float32),
        in_specs=[vmem, vmem],
        out_specs=vmem,
        compiler_params=pltpu.CompilerParams(vmem_limit_bytes=8 * 2**20),
        name="project",
    )(inverse, pieces)


def shift(array, axis, size, by):
    return lax.ppermute(array, axis, [(i, (i + by) % size) for i in range(size)])


def body(slab, test_matrix):
    place = lax.axis_index("c").astype(jnp.int32).reshape(1)
    slab = pltpu.with_memory_space_constraint(slab, pltpu.HBM)
    test_matrix = pltpu.with_memory_space_constraint(test_matrix, pltpu.HBM)
    gram, mine, other = sketch_call(place, slab, test_matrix)
    gram = gram + shift(gram, "c", 2, 1)
    half = mine + shift(other, "c", 2, 1)
    half, gram = lax.optimization_barrier((half, gram))
    part = jnp.sum(lax.all_to_all(half, "x", 0, 0, tiled=True), axis=0)
    for axis in ("z", "y", "x"):
        ahead, behind, across = (shift(gram, axis, 4, by) for by in (1, -1, 2))
        gram = (gram + across) + (ahead + behind)
    pieces = lax.all_to_all(part, ("y", "z"), 0, 0, tiled=True)
    return project_call(factor_call(gram), pieces).T


def solution(mesh):
    grid = Mesh(mesh.devices.reshape(4, 4, 4, 2), AXES)
    return jax.shard_map(
        body, mesh=grid, in_specs=(P(AXES, None), P()), out_specs=P(None, AXES), check_vma=False
    )
```

```python
import jax
import jax.numpy as jnp
from jax import lax
from jax.experimental import pallas as pl
from jax.experimental.pallas import tpu as pltpu
from jax.sharding import PartitionSpec as P

SIDE = 4
K = 128
CHUNK = 256
AHEAD = 3
COLS = 512
NT = (((1,), (1,)), ((), ()))


def place_of(chip):
    return chip // SIDE**2, chip // SIDE % SIDE, chip % SIDE


def turn(target, here):
    apart = target ^ here
    return 2 * ((apart >> 1) ^ (apart & 1)) + (apart >> 1)


def device(y, z, x, core):
    return ((y * SIDE + z) * SIDE + x) * 2 + core


def sketch_kernel(place_ref, slab_ref, omega_ref, gram_ref, mine_ref, other_ref, slab_v, omega_v, beside, above, sems, omega_sem):
    rows, width = slab_v.shape
    chunks = rows // CHUNK

    def copy(i):
        at = pl.ds(i * CHUNK, CHUNK)
        return pltpu.make_async_copy(slab_ref.at[at, :], slab_v.at[at, :], sems.at[i])

    def split(value):
        high = value.astype(jnp.bfloat16)
        return high, (value - high.astype(jnp.float32)).astype(jnp.bfloat16)

    omega_copy = pltpu.make_async_copy(omega_ref, omega_v, omega_sem)
    omega_copy.start()
    copy(0).start()
    omega_copy.wait()
    for i in range(1, AHEAD):
        copy(i).start()
    for i in range(chunks):
        copy(i).wait()
        if i + AHEAD < chunks:
            copy(i + AHEAD).start()
        at = pl.ds(i * CHUNK, CHUNK)
        sketch = jnp.dot(slab_v[at, :], omega_v[...], preferred_element_type=jnp.float32)
        beside[at, :K], beside[at, K:] = split(sketch)
        above[:K, at], above[K:, at] = split(sketch.T)
    gram = jnp.dot(above[...], beside[...], preferred_element_type=jnp.float32)
    gram_ref[...] = (gram[K:, K:] + (gram[:K, K:] + gram[K:, :K])) + gram[:K, :K]

    y, z, x, core = (place_ref[i] for i in range(4))
    first = core == 0
    for n in range(width // COLS):
        both = jnp.dot(above[...], slab_v[:, pl.ds(n * COLS, COLS)], preferred_element_type=jnp.float32)
        tile = (both[K:, :] + both[:K, :]).T.reshape(COLS // 64, 2, 32, K)
        for chip in range(COLS // 64):
            to_y, to_z, to_x = place_of(n * (COLS // 64) + chip)
            even, odd = tile[chip, 0], tile[chip, 1]
            by_y, by_z, by_x = turn(to_y, y), turn(to_z, z), turn(to_x, x)
            mine_at = jnp.where(first, by_x, by_z), SIDE * jnp.where(first, by_z, by_x) + by_y
            other_at = jnp.where(first, by_z, by_x), SIDE * jnp.where(first, by_x, by_z) + by_y
            mine_ref[mine_at[0], mine_at[1]] = jnp.where(first, even, odd)
            other_ref[other_at[0], other_at[1]] = jnp.where(first, odd, even)


def sketch_call(place, slab, omega):
    rows, width = slab.shape
    vmem = pl.BlockSpec(memory_space=pltpu.VMEM)
    hbm = pl.BlockSpec(memory_space=pltpu.HBM)
    half = jax.ShapeDtypeStruct((SIDE, SIDE * SIDE, 32, K), jnp.float32)
    return pl.pallas_call(
        sketch_kernel,
        out_shape=(jax.ShapeDtypeStruct((K, K), jnp.float32), half, half),
        in_specs=[pl.BlockSpec(memory_space=pltpu.SMEM), hbm, hbm],
        out_specs=(vmem,) * 3,
        scratch_shapes=[
            pltpu.VMEM((rows, width), slab.dtype),
            pltpu.VMEM(omega.shape, omega.dtype),
            pltpu.VMEM((rows, 2 * K), jnp.bfloat16),
            pltpu.VMEM((2 * K, rows), jnp.bfloat16),
            pltpu.SemaphoreType.DMA((rows // CHUNK,)),
            pltpu.SemaphoreType.DMA,
        ],
        compiler_params=pltpu.CompilerParams(vmem_limit_bytes=36 * 2**20),
        cost_estimate=pl.CostEstimate(
            flops=2 * rows * width * 3 * K, bytes_accessed=2 * rows * width, transcendentals=0
        ),
        name="sketch",
    )(place, slab, omega)


def factor_rows(blocks):
    shape = (8, K)
    lane = lax.broadcasted_iota(jnp.int32, shape, 1)
    sublane = lax.broadcasted_iota(jnp.int32, shape, 0)
    blocks = list(blocks)
    count = len(blocks)
    done = []

    def column(array, at):
        return jnp.broadcast_to(array[:, at : at + 1], shape)

    def row(array, at):
        return jnp.broadcast_to(array[at : at + 1, :], shape)

    for b in range(count):
        first = 8 * b
        inside = (lane >= first) & (lane < first + 8)
        columns = [column(blocks[b], first + k) for k in range(8)]
        entry = {(i, k): row(columns[k], i) for k in range(8) for i in range(k, 8)}
        cleared = jnp.where(inside, (lane - first == sublane).astype(jnp.float32), blocks[b])
        rows = [row(cleared, k) for k in range(8)]
        inverse = [None] * 8
        lower = {}
        for k in range(8):
            inverse[k] = pltpu.reciprocal(entry[k, k], approx=True)
            for i in range(k + 1, 8):
                lower[i, k] = entry[i, k] * inverse[k]
            for i in range(k + 1, 8):
                for j in range(k + 1, i + 1):
                    entry[i, j] = entry[i, j] - lower[i, k] * entry[j, k]
        for k in range(8):
            for m in range(k):
                rows[k] = rows[k] - lower[k, m] * rows[m]
        result = jnp.zeros(shape, jnp.float32)
        for k in range(8):
            result = jnp.where(sublane == k, rows[k] * lax.rsqrt(entry[k, k]), result)
        done.append(jnp.where(lane <= first + sublane, result, 0.0))
        if b + 1 == count:
            break
        target = blocks[b + 1]
        factors = [column(target, first + k) for k in range(8)]
        target = jnp.where(inside, 0.0, target)
        for k in range(8):
            factor = factors[k] * inverse[k]
            for m in range(k + 1, 8):
                factors[m] = factors[m] - factor * entry[m, k]
            target = target - factor * rows[k]
        blocks[b + 1] = target
        solved = [None] * 8
        for k in reversed(range(8)):
            value = rows[k] * inverse[k]
            for m in range(k + 1, 8):
                value = value - lower[m, k] * solved[m]
            solved[k] = value
        for i in range(b + 2, count):
            products = [column(blocks[i], first + k) * solved[k] for k in range(8)]
            while len(products) > 1:
                products = [products[p] + products[p + 1] for p in range(0, len(products), 2)]
            blocks[i] = jnp.where(inside, 0.0, blocks[i]) - products[0]
    return done


def factor_kernel(gram_ref, inverse_ref):
    blocks = [gram_ref[pl.ds(8 * b, 8), :] for b in range(K // 8)]
    for b, rows in enumerate(factor_rows(blocks)):
        inverse_ref[pl.ds(8 * b, 8), :] = rows


def factor_call(gram):
    vmem = pl.BlockSpec(memory_space=pltpu.VMEM)
    return pl.pallas_call(
        factor_kernel,
        out_shape=jax.ShapeDtypeStruct((K, K), jnp.float32),
        in_specs=[vmem],
        out_specs=vmem,
        compiler_params=pltpu.CompilerParams(vmem_limit_bytes=8 * 2**20),
        cost_estimate=pl.CostEstimate(flops=5 * 10**10, bytes_accessed=2**17, transcendentals=0),
        name="factor",
    )(gram)


def project_kernel(inverse_ref, pieces_ref, out_ref):
    total = jnp.sum(pieces_ref[...], axis=0)
    out_ref[...] = lax.dot_general(
        total, inverse_ref[...], NT, precision=lax.Precision.HIGHEST, preferred_element_type=jnp.float32
    )


def project_call(inverse, pieces):
    vmem = pl.BlockSpec(memory_space=pltpu.VMEM)
    return pl.pallas_call(
        project_kernel,
        out_shape=jax.ShapeDtypeStruct((pieces.shape[1], K), jnp.float32),
        in_specs=[vmem, vmem],
        out_specs=vmem,
        compiler_params=pltpu.CompilerParams(vmem_limit_bytes=8 * 2**20),
        name="project",
    )(inverse, pieces)


def swap_cores(array):
    return lax.ppermute(array, "rows", [(i, i ^ 1) for i in range(2 * SIDE**3)])


def swap_chips(array, axes, mask):
    pairs = []
    for chip in range(SIDE**3):
        for core in range(2):
            target = list(place_of(chip))
            target[axes[core]] ^= mask
            pairs.append((2 * chip + core, device(*target, core)))
    return lax.ppermute(array, "rows", pairs)


def body(slab, test_matrix):
    me = lax.axis_index("rows").astype(jnp.int32)
    place = jnp.stack([*place_of(me // 2), me % 2])
    slab = pltpu.with_memory_space_constraint(slab, pltpu.HBM)
    test_matrix = pltpu.with_memory_space_constraint(test_matrix, pltpu.HBM)
    gram, mine, other = sketch_call(place, slab, test_matrix)

    pieces = SIDE**3
    mine, other = mine.reshape(pieces, 32, K), other.reshape(pieces, 32, K)
    gram = gram.reshape(-1, 32, K)
    got = swap_cores(jnp.concatenate([other, gram]))
    part, gram = mine + got[:pieces], gram + got[pieces:]
    for axes in ((2, 1), (1, 2), (0, 0)):
        pieces //= 4
        quarters = [part[i * pieces : (i + 1) * pieces] for i in range(4)]
        got = [
            swap_chips(jnp.concatenate([quarters[i], gram]), axes, mask) for i, mask in ((3, 2), (1, 3), (2, 1))
        ]
        part = (quarters[0] + got[0][:pieces]) + (got[1][:pieces] + got[2][:pieces])
        gram = (gram + got[0][pieces:]) + (got[1][pieces:] + got[2][pieces:])
    return project_call(factor_call(gram.reshape(K, K)), part).T


def solution(mesh):
    return jax.shard_map(
        body, mesh=mesh, in_specs=(P("rows", None), P()), out_specs=P(None, "rows"), check_vma=False
    )
```

```python
import jax
import jax.numpy as jnp
from jax import lax
from jax.experimental import pallas as pl
from jax.experimental.pallas import tpu as pltpu
from jax.sharding import PartitionSpec as P

SIDE = 4
K = 128
CHUNK = 256
AHEAD = 4
COLS = 512
NT = (((1,), (1,)), ((), ()))


def place_of(chip):
    return chip // SIDE**2, chip // SIDE % SIDE, chip % SIDE


def turn(target, here):
    apart = target ^ here
    return 2 * ((apart >> 1) ^ (apart & 1)) + (apart >> 1)


def device(y, z, x, core):
    return ((y * SIDE + z) * SIDE + x) * 2 + core


def lanes(rows):
    return lax.broadcasted_iota(jnp.int32, (rows, K), 1)


def pack(gram):
    third = jnp.where(lanes(32) < 96, gram[64:96], pltpu.roll(gram[:32], 96, 1))
    second = jnp.where(lanes(16) < 64, gram[32:48], pltpu.roll(gram[48:64], 64, 1))
    return jnp.concatenate([gram[96:], third, second], axis=0)


def unpack(packed):
    third, second = packed[32:64], packed[64:80]
    low = [pltpu.roll(third, 32, 1), second, pltpu.roll(second, 64, 1), third, packed[:32]]
    low = jnp.concatenate(low, axis=0)
    row = lax.broadcasted_iota(jnp.int32, (K, K), 0)
    return jnp.where(row // 32 >= lanes(K) // 32, low, low.T)


def sketch_kernel(place_ref, slab_ref, omega_ref, gram_ref, mine_ref, other_ref, slab_v, omega_v, beside, above, sems, omega_sem):
    rows, width = slab_v.shape
    chunks = rows // CHUNK

    def copy(i):
        at = pl.ds(i * CHUNK, CHUNK)
        return pltpu.make_async_copy(slab_ref.at[at, :], slab_v.at[at, :], sems.at[i])

    def split(value):
        high = value.astype(jnp.bfloat16)
        return high, (value - high.astype(jnp.float32)).astype(jnp.bfloat16)

    omega_copy = pltpu.make_async_copy(omega_ref, omega_v, omega_sem)
    omega_copy.start()
    copy(0).start()
    omega_copy.wait()
    for i in range(1, AHEAD):
        copy(i).start()
    def keep(i, sketch):
        at = pl.ds(i * CHUNK, CHUNK)
        beside[at, :K], beside[at, K:] = split(sketch)
        above[:K, at], above[K:, at] = split(sketch.T)

    last = None
    for i in range(chunks):
        copy(i).wait()
        if i + AHEAD < chunks:
            copy(i + AHEAD).start()
        block = slab_v[pl.ds(i * CHUNK, CHUNK), :]
        sketch = jnp.dot(block, omega_v[...], preferred_element_type=jnp.float32)
        if i > 0:
            keep(i - 1, last)
        last = sketch
    keep(chunks - 1, last)
    gram = jnp.dot(above[...], beside[...], preferred_element_type=jnp.float32)
    gram_ref[...] = pack((gram[K:, K:] + (gram[:K, K:] + gram[K:, :K])) + gram[:K, :K])

    y, z, x, core = (place_ref[i] for i in range(4))
    first = core == 0
    for n in range(width // COLS):
        both = jnp.dot(above[...], slab_v[:, pl.ds(n * COLS, COLS)], preferred_element_type=jnp.float32)
        tile = (both[K:, :] + both[:K, :]).T.reshape(COLS // 64, 2, 32, K)
        for chip in range(COLS // 64):
            to_y, to_z, to_x = place_of(n * (COLS // 64) + chip)
            even, odd = tile[chip, 0], tile[chip, 1]
            by_y, by_z, by_x = turn(to_y, y), turn(to_z, z), turn(to_x, x)
            even_at = by_x, SIDE * by_z + by_y
            odd_at = by_z, SIDE * by_x + by_y
            mine_at = [jnp.where(first, p, q) for p, q in zip(even_at, odd_at)]
            other_at = [jnp.where(first, q, p) for p, q in zip(even_at, odd_at)]
            mine_ref[mine_at[0], mine_at[1]] = jnp.where(first, even, odd)
            other_ref[other_at[0], other_at[1]] = jnp.where(first, odd, even)


def sketch_call(place, slab, omega):
    rows, width = slab.shape
    vmem = pl.BlockSpec(memory_space=pltpu.VMEM)
    hbm = pl.BlockSpec(memory_space=pltpu.HBM)
    half = jax.ShapeDtypeStruct((SIDE, SIDE * SIDE, 32, K), jnp.float32)
    return pl.pallas_call(
        sketch_kernel,
        out_shape=(jax.ShapeDtypeStruct((80, K), jnp.float32), half, half),
        in_specs=[pl.BlockSpec(memory_space=pltpu.SMEM), hbm, hbm],
        out_specs=(vmem,) * 3,
        scratch_shapes=[
            pltpu.VMEM((rows, width), slab.dtype),
            pltpu.VMEM(omega.shape, omega.dtype),
            pltpu.VMEM((rows, 2 * K), jnp.bfloat16),
            pltpu.VMEM((2 * K, rows), jnp.bfloat16),
            pltpu.SemaphoreType.DMA((rows // CHUNK,)),
            pltpu.SemaphoreType.DMA,
        ],
        compiler_params=pltpu.CompilerParams(vmem_limit_bytes=36 * 2**20),
        cost_estimate=pl.CostEstimate(
            flops=2 * rows * width * 3 * K, bytes_accessed=2 * rows * width, transcendentals=0
        ),
        name="sketch",
    )(place, slab, omega)


AXES = (2, 1), (1, 2), (0, 0)
MASKS = 3, 1, 2


def factor_rows(blocks):
    shape = (8, K)
    lane = lax.broadcasted_iota(jnp.int32, shape, 1)
    sublane = lax.broadcasted_iota(jnp.int32, shape, 0)
    blocks = list(blocks)
    count = len(blocks)
    done = []

    def column(array, at):
        return jnp.broadcast_to(array[:, at : at + 1], shape)

    def row(array, at):
        return jnp.broadcast_to(array[at : at + 1, :], shape)

    for b in range(count):
        first = 8 * b
        inside = (lane >= first) & (lane < first + 8)
        columns = [column(blocks[b], first + k) for k in range(8)]
        entry = {(i, k): row(columns[k], i) for k in range(8) for i in range(k, 8)}
        cleared = jnp.where(inside, (lane - first == sublane).astype(jnp.float32), blocks[b])
        rows = [row(cleared, k) for k in range(8)]
        inverse = [None] * 8
        lower = {}
        for k in range(8):
            inverse[k] = pltpu.reciprocal(entry[k, k], approx=True)
            for i in range(k + 1, 8):
                lower[i, k] = entry[i, k] * inverse[k]
            for i in range(k + 1, 8):
                for j in range(k + 1, i + 1):
                    entry[i, j] = entry[i, j] - lower[i, k] * entry[j, k]
        for k in range(8):
            for m in range(k):
                rows[k] = rows[k] - lower[k, m] * rows[m]
        result = jnp.zeros(shape, jnp.float32)
        for k in range(8):
            result = jnp.where(sublane == k, rows[k] * lax.rsqrt(entry[k, k]), result)
        done.append(jnp.where(lane <= first + sublane, result, 0.0))
        if b + 1 == count:
            break
        target = blocks[b + 1]
        factors = [column(target, first + k) for k in range(8)]
        target = jnp.where(inside, 0.0, target)
        for k in range(8):
            factor = factors[k] * inverse[k]
            for m in range(k + 1, 8):
                factors[m] = factors[m] - factor * entry[m, k]
            target = target - factor * rows[k]
        blocks[b + 1] = target
        solved = [None] * 8
        for k in reversed(range(8)):
            value = rows[k] * inverse[k]
            for m in range(k + 1, 8):
                value = value - lower[m, k] * solved[m]
            solved[k] = value
        for i in range(b + 2, count):
            products = [column(blocks[i], first + k) * solved[k] for k in range(8)]
            while len(products) > 1:
                products = [products[p] + products[p + 1] for p in range(0, len(products), 2)]
            blocks[i] = jnp.where(inside, 0.0, blocks[i]) - products[0]
    return done


def finish_kernel(part_ref, gram_ref, near_ref, other_ref, across_ref, out_ref, inverse):
    columns = part_ref.shape[0]
    own = jnp.concatenate([part_ref[...], gram_ref[...]], axis=0)
    total = (own + across_ref[...]) + (near_ref[...] + other_ref[...])
    gram = unpack(total[columns:])
    for b, rows in enumerate(factor_rows([gram[8 * b : 8 * b + 8] for b in range(K // 8)])):
        inverse[pl.ds(8 * b, 8), :] = rows
    out_ref[...] = lax.dot_general(
        total[:columns], inverse[...], NT, precision=lax.Precision.HIGHEST, preferred_element_type=jnp.float32
    )


def finish_call(part, gram, got):
    vmem = pl.BlockSpec(memory_space=pltpu.VMEM)
    return pl.pallas_call(
        finish_kernel,
        out_shape=jax.ShapeDtypeStruct(part.shape, jnp.float32),
        in_specs=[vmem] * 5,
        out_specs=vmem,
        scratch_shapes=[pltpu.VMEM((K, K), jnp.float32)],
        compiler_params=pltpu.CompilerParams(vmem_limit_bytes=8 * 2**20),
        cost_estimate=pl.CostEstimate(flops=10**9, bytes_accessed=2**20, transcendentals=0),
        name="finish",
    )(part, gram, *got)


def swap_cores(array):
    return lax.ppermute(array, "rows", [(i, i ^ 1) for i in range(2 * SIDE**3)])


def swap_chips(array, axes, mask):
    pairs = []
    for chip in range(SIDE**3):
        for core, axis in enumerate(axes):
            target = list(place_of(chip))
            target[axis] ^= mask
            pairs.append((2 * chip + core, device(*target, core)))
    return lax.ppermute(array, "rows", pairs)


def body(slab, test_matrix):
    me = lax.axis_index("rows").astype(jnp.int32)
    place = jnp.stack([*place_of(me // 2), me % 2])
    slab = pltpu.with_memory_space_constraint(slab, pltpu.HBM)
    test_matrix = pltpu.with_memory_space_constraint(test_matrix, pltpu.HBM)
    gram, mine, other = sketch_call(place, slab, test_matrix)

    rows = SIDE**3 * 32
    mine, other = mine.reshape(rows, K), other.reshape(rows, K)
    got = swap_cores(jnp.concatenate([other, gram]))
    part, gram = mine + got[:rows], gram + got[rows:]
    for number, axes in enumerate(AXES):
        rows //= 4
        stay, *leave = (part[i * rows : (i + 1) * rows] for i in range(4))
        got = [swap_chips(jnp.concatenate([piece, gram]), axes, mask) for piece, mask in zip(leave, MASKS)]
        if number + 1 == len(AXES):
            return finish_call(stay, gram, got).T
        part = (stay + got[2][:rows]) + (got[0][:rows] + got[1][:rows])
        gram = (gram + got[2][rows:]) + (got[0][rows:] + got[1][rows:])


def solution(mesh):
    return jax.shard_map(
        body, mesh=mesh, in_specs=(P("rows", None), P()), out_specs=P(None, "rows"), check_vma=False
    )
```

```python
import jax
import jax.numpy as jnp
from jax import lax
from jax.experimental import pallas as pl
from jax.experimental.pallas import tpu as pltpu
from jax.sharding import PartitionSpec as P

SIDE = 4
K = 128
CHUNK = 256
AHEAD = 4
COLS = 512
NT = (((1,), (1,)), ((), ()))


def place_of(chip):
    return chip // SIDE**2, chip // SIDE % SIDE, chip % SIDE


def turn(target, here):
    apart = target ^ here
    return 2 * ((apart >> 1) ^ (apart & 1)) + (apart >> 1)


def device(y, z, x, core):
    return ((y * SIDE + z) * SIDE + x) * 2 + core


def lanes(rows):
    return lax.broadcasted_iota(jnp.int32, (rows, K), 1)


def pack(gram):
    third = jnp.where(lanes(32) < 96, gram[64:96], pltpu.roll(gram[:32], 96, 1))
    second = jnp.where(lanes(16) < 64, gram[32:48], pltpu.roll(gram[48:64], 64, 1))
    return jnp.concatenate([gram[96:], third, second], axis=0)


def unpack(packed):
    third, second = packed[32:64], packed[64:80]
    low = [pltpu.roll(third, 32, 1), second, pltpu.roll(second, 64, 1), third, packed[:32]]
    low = jnp.concatenate(low, axis=0)
    row = lax.broadcasted_iota(jnp.int32, (K, K), 0)
    return jnp.where(row // 32 >= lanes(K) // 32, low, low.T)


def sketch_kernel(place_ref, slab_ref, omega_ref, gram_ref, mine_ref, other_ref, slab_v, omega_v, beside, above, sems, omega_sem):
    rows, width = slab_v.shape
    chunks = rows // CHUNK

    def copy(i):
        at = pl.ds(i * CHUNK, CHUNK)
        return pltpu.make_async_copy(slab_ref.at[at, :], slab_v.at[at, :], sems.at[i])

    def split(value):
        high = value.astype(jnp.bfloat16)
        return high, (value - high.astype(jnp.float32)).astype(jnp.bfloat16)

    omega_copy = pltpu.make_async_copy(omega_ref, omega_v, omega_sem)
    omega_copy.start()
    copy(0).start()
    omega_copy.wait()
    for i in range(1, AHEAD):
        copy(i).start()
    def keep(i, sketch):
        at = pl.ds(i * CHUNK, CHUNK)
        beside[at, :K], beside[at, K:] = split(sketch)
        above[:K, at], above[K:, at] = split(sketch.T)

    last = None
    for i in range(chunks):
        copy(i).wait()
        if i + AHEAD < chunks:
            copy(i + AHEAD).start()
        block = slab_v[pl.ds(i * CHUNK, CHUNK), :]
        sketch = jnp.dot(block, omega_v[...], preferred_element_type=jnp.float32)
        if i > 0:
            keep(i - 1, last)
        last = sketch
    keep(chunks - 1, last)
    gram = jnp.dot(above[...], beside[...], preferred_element_type=jnp.float32)
    gram_ref[...] = pack((gram[K:, K:] + (gram[:K, K:] + gram[K:, :K])) + gram[:K, :K])

    y, z, x, core = (place_ref[i] for i in range(4))
    first = core == 0
    for n in range(width // COLS):
        both = jnp.dot(above[...], slab_v[:, pl.ds(n * COLS, COLS)], preferred_element_type=jnp.float32)
        tile = (both[K:, :] + both[:K, :]).T.reshape(COLS // 64, 2, 32, K)
        for chip in range(COLS // 64):
            to_y, to_z, to_x = place_of(n * (COLS // 64) + chip)
            even, odd = tile[chip, 0], tile[chip, 1]
            by_y, by_z, by_x = turn(to_y, y), turn(to_z, z), turn(to_x, x)
            even_at = by_x, SIDE * by_z + by_y
            odd_at = by_z, SIDE * by_x + by_y
            mine_at = [jnp.where(first, p, q) for p, q in zip(even_at, odd_at)]
            other_at = [jnp.where(first, q, p) for p, q in zip(even_at, odd_at)]
            mine_ref[mine_at[0], mine_at[1]] = jnp.where(first, even, odd)
            other_ref[other_at[0], other_at[1]] = jnp.where(first, odd, even)


def sketch_call(place, slab, omega):
    rows, width = slab.shape
    vmem = pl.BlockSpec(memory_space=pltpu.VMEM)
    hbm = pl.BlockSpec(memory_space=pltpu.HBM)
    half = jax.ShapeDtypeStruct((SIDE, SIDE * SIDE, 32, K), jnp.float32)
    return pl.pallas_call(
        sketch_kernel,
        out_shape=(jax.ShapeDtypeStruct((80, K), jnp.float32), half, half),
        in_specs=[pl.BlockSpec(memory_space=pltpu.SMEM), hbm, hbm],
        out_specs=(vmem,) * 3,
        scratch_shapes=[
            pltpu.VMEM((rows, width), slab.dtype),
            pltpu.VMEM(omega.shape, omega.dtype),
            pltpu.VMEM((rows, 2 * K), jnp.bfloat16),
            pltpu.VMEM((2 * K, rows), jnp.bfloat16),
            pltpu.SemaphoreType.DMA((rows // CHUNK,)),
            pltpu.SemaphoreType.DMA,
        ],
        compiler_params=pltpu.CompilerParams(vmem_limit_bytes=36 * 2**20),
        cost_estimate=pl.CostEstimate(
            flops=2 * rows * width * 3 * K, bytes_accessed=2 * rows * width, transcendentals=0
        ),
        name="sketch",
    )(place, slab, omega)


AXES = (2, 1), (1, 2), (0, 0)
MASKS = 3, 1, 2


def factor_rows(blocks):
    shape = (8, K)
    lane = lax.broadcasted_iota(jnp.int32, shape, 1)
    sublane = lax.broadcasted_iota(jnp.int32, shape, 0)
    blocks = list(blocks)
    count = len(blocks)
    done = []

    def column(array, at):
        return jnp.broadcast_to(array[:, at : at + 1], shape)

    def row(array, at):
        return jnp.broadcast_to(array[at : at + 1, :], shape)

    for b in range(count):
        first = 8 * b
        inside = (lane >= first) & (lane < first + 8)
        columns = [column(blocks[b], first + k) for k in range(8)]
        entry = {(i, k): row(columns[k], i) for k in range(8) for i in range(k, 8)}
        cleared = jnp.where(inside, (lane - first == sublane).astype(jnp.float32), blocks[b])
        rows = [row(cleared, k) for k in range(8)]
        inverse = [None] * 8
        lower = {}
        for k in range(8):
            inverse[k] = pltpu.reciprocal(entry[k, k], approx=True)
            for i in range(k + 1, 8):
                lower[i, k] = entry[i, k] * inverse[k]
            for i in range(k + 1, 8):
                for j in range(k + 1, i + 1):
                    entry[i, j] = entry[i, j] - lower[i, k] * entry[j, k]
        for k in range(8):
            for m in range(k):
                rows[k] = rows[k] - lower[k, m] * rows[m]
        result = jnp.zeros(shape, jnp.float32)
        for k in range(8):
            result = jnp.where(sublane == k, rows[k] * lax.rsqrt(entry[k, k]), result)
        done.append(jnp.where(lane <= first + sublane, result, 0.0))
        if b + 1 == count:
            break
        for i in range(b + 1, count):
            target = blocks[i]
            factors = [column(target, first + k) for k in range(8)]
            target = jnp.where(inside, 0.0, target)
            for k in range(8):
                factor = factors[k] * inverse[k]
                for m in range(k + 1, 8):
                    factors[m] = factors[m] - factor * entry[m, k]
                target = target - factor * rows[k]
            blocks[i] = target
    return done


def finish_kernel(part_ref, gram_ref, near_ref, other_ref, across_ref, out_ref, inverse):
    columns = part_ref.shape[0]
    own = jnp.concatenate([part_ref[...], gram_ref[...]], axis=0)
    total = (own + across_ref[...]) + (near_ref[...] + other_ref[...])
    gram = unpack(total[columns:])
    for b, rows in enumerate(factor_rows([gram[8 * b : 8 * b + 8] for b in range(K // 8)])):
        inverse[pl.ds(8 * b, 8), :] = rows
    out_ref[...] = lax.dot_general(
        total[:columns], inverse[...], NT, precision=lax.Precision.HIGHEST, preferred_element_type=jnp.float32
    )


def finish_call(part, gram, got):
    vmem = pl.BlockSpec(memory_space=pltpu.VMEM)
    return pl.pallas_call(
        finish_kernel,
        out_shape=jax.ShapeDtypeStruct(part.shape, jnp.float32),
        in_specs=[vmem] * 5,
        out_specs=vmem,
        scratch_shapes=[pltpu.VMEM((K, K), jnp.float32)],
        compiler_params=pltpu.CompilerParams(vmem_limit_bytes=8 * 2**20),
        cost_estimate=pl.CostEstimate(flops=10**9, bytes_accessed=2**20, transcendentals=0),
        name="finish",
    )(part, gram, *got)


def swap_cores(array):
    return lax.ppermute(array, "rows", [(i, i ^ 1) for i in range(2 * SIDE**3)])


def swap_chips(array, axes, mask):
    pairs = []
    for chip in range(SIDE**3):
        for core, axis in enumerate(axes):
            target = list(place_of(chip))
            target[axis] ^= mask
            pairs.append((2 * chip + core, device(*target, core)))
    return lax.ppermute(array, "rows", pairs)


def body(slab, test_matrix):
    me = lax.axis_index("rows").astype(jnp.int32)
    place = jnp.stack([*place_of(me // 2), me % 2])
    slab = pltpu.with_memory_space_constraint(slab, pltpu.HBM)
    test_matrix = pltpu.with_memory_space_constraint(test_matrix, pltpu.HBM)
    gram, mine, other = sketch_call(place, slab, test_matrix)

    rows = SIDE**3 * 32
    mine, other = mine.reshape(rows, K), other.reshape(rows, K)
    got = swap_cores(jnp.concatenate([other, gram]))
    part, gram = mine + got[:rows], gram + got[rows:]
    for number, axes in enumerate(AXES):
        rows //= 4
        stay, *leave = (part[i * rows : (i + 1) * rows] for i in range(4))
        got = [swap_chips(jnp.concatenate([piece, gram]), axes, mask) for piece, mask in zip(leave, MASKS)]
        if number + 1 == len(AXES):
            return finish_call(stay, gram, got).T
        part = (stay + got[2][:rows]) + (got[0][:rows] + got[1][:rows])
        gram = (gram + got[2][rows:]) + (got[0][rows:] + got[1][rows:])


def solution(mesh):
    return jax.shard_map(
        body, mesh=mesh, in_specs=(P("rows", None), P()), out_specs=P(None, "rows"), check_vma=False
    )
```

```python
import jax
import jax.numpy as jnp
from jax import lax
from jax.experimental import pallas as pl
from jax.experimental.pallas import tpu as pltpu
from jax.sharding import PartitionSpec as P

SIDE = 4
K = 128
CHUNK = 256
AHEAD = 4
COLS = 512
NT = (((1,), (1,)), ((), ()))


def place_of(chip):
    return chip // SIDE**2, chip // SIDE % SIDE, chip % SIDE


def turn(target, here):
    apart = target ^ here
    return 2 * ((apart >> 1) ^ (apart & 1)) + (apart >> 1)


def device(y, z, x, core):
    return ((y * SIDE + z) * SIDE + x) * 2 + core


def lanes(rows):
    return lax.broadcasted_iota(jnp.int32, (rows, K), 1)


def pack(gram):
    third = jnp.where(lanes(32) < 96, gram[64:96], pltpu.roll(gram[:32], 96, 1))
    second = jnp.where(lanes(16) < 64, gram[32:48], pltpu.roll(gram[48:64], 64, 1))
    return jnp.concatenate([gram[96:], third, second], axis=0)


def unpack(packed):
    third, second = packed[32:64], packed[64:80]
    low = [pltpu.roll(third, 32, 1), second, pltpu.roll(second, 64, 1), third, packed[:32]]
    low = jnp.concatenate(low, axis=0)
    row = lax.broadcasted_iota(jnp.int32, (K, K), 0)
    return jnp.where(row // 32 >= lanes(K) // 32, low, low.T)


def sketch_kernel(place_ref, slab_ref, omega_ref, gram_ref, mine_ref, other_ref, slab_v, omega_v, beside, above, sems, omega_sem):
    rows, width = slab_v.shape
    chunks = rows // CHUNK

    def copy(i):
        at = pl.ds(i * CHUNK, CHUNK)
        return pltpu.make_async_copy(slab_ref.at[at, :], slab_v.at[at, :], sems.at[i])

    def split(value):
        high = value.astype(jnp.bfloat16)
        return high, (value - high.astype(jnp.float32)).astype(jnp.bfloat16)

    omega_copy = pltpu.make_async_copy(omega_ref, omega_v, omega_sem)
    omega_copy.start()
    copy(0).start()
    omega_copy.wait()
    for i in range(1, AHEAD):
        copy(i).start()
    def keep(i, sketch):
        at = pl.ds(i * CHUNK, CHUNK)
        beside[at, :K], beside[at, K:] = split(sketch)
        above[:K, at], above[K:, at] = split(sketch.T)

    last = None
    for i in range(chunks):
        copy(i).wait()
        if i + AHEAD < chunks:
            copy(i + AHEAD).start()
        block = slab_v[pl.ds(i * CHUNK, CHUNK), :]
        sketch = jnp.dot(block, omega_v[...], preferred_element_type=jnp.float32)
        if i > 0:
            keep(i - 1, last)
        last = sketch
    keep(chunks - 1, last)
    gram = jnp.dot(above[...], beside[...], preferred_element_type=jnp.float32)
    gram_ref[...] = pack((gram[K:, K:] + (gram[:K, K:] + gram[K:, :K])) + gram[:K, :K])

    y, z, x, core = (place_ref[i] for i in range(4))
    first = core == 0
    for n in range(width // COLS):
        both = jnp.dot(above[...], slab_v[:, pl.ds(n * COLS, COLS)], preferred_element_type=jnp.float32)
        tile = (both[K:, :] + both[:K, :]).T.reshape(COLS // 64, 2, 32, K)
        for chip in range(COLS // 64):
            to_y, to_z, to_x = place_of(n * (COLS // 64) + chip)
            even, odd = tile[chip, 0], tile[chip, 1]
            by_y, by_z, by_x = turn(to_y, y), turn(to_z, z), turn(to_x, x)
            even_at = by_x, SIDE * by_z + by_y
            odd_at = by_z, SIDE * by_y + by_x
            mine_at = [jnp.where(first, p, q) for p, q in zip(even_at, odd_at)]
            other_at = [jnp.where(first, q, p) for p, q in zip(even_at, odd_at)]
            mine_ref[mine_at[0], mine_at[1]] = jnp.where(first, even, odd)
            other_ref[other_at[0], other_at[1]] = jnp.where(first, odd, even)


def sketch_call(place, slab, omega):
    rows, width = slab.shape
    vmem = pl.BlockSpec(memory_space=pltpu.VMEM)
    hbm = pl.BlockSpec(memory_space=pltpu.HBM)
    half = jax.ShapeDtypeStruct((SIDE, SIDE * SIDE, 32, K), jnp.float32)
    return pl.pallas_call(
        sketch_kernel,
        out_shape=(jax.ShapeDtypeStruct((80, K), jnp.float32), half, half),
        in_specs=[pl.BlockSpec(memory_space=pltpu.SMEM), hbm, hbm],
        out_specs=(vmem,) * 3,
        scratch_shapes=[
            pltpu.VMEM((rows, width), slab.dtype),
            pltpu.VMEM(omega.shape, omega.dtype),
            pltpu.VMEM((rows, 2 * K), jnp.bfloat16),
            pltpu.VMEM((2 * K, rows), jnp.bfloat16),
            pltpu.SemaphoreType.DMA((rows // CHUNK,)),
            pltpu.SemaphoreType.DMA,
        ],
        compiler_params=pltpu.CompilerParams(vmem_limit_bytes=36 * 2**20),
        cost_estimate=pl.CostEstimate(
            flops=2 * rows * width * 3 * K, bytes_accessed=2 * rows * width, transcendentals=0
        ),
        name="sketch",
    )(place, slab, omega)


AXES = (2, 1), (1, 0), (0, 2)
MASKS = 3, 1, 2


def factor_rows(blocks):
    shape = (8, K)
    lane = lax.broadcasted_iota(jnp.int32, shape, 1)
    sublane = lax.broadcasted_iota(jnp.int32, shape, 0)
    blocks = list(blocks)
    count = len(blocks)
    done = []

    def column(array, at):
        return jnp.broadcast_to(array[:, at : at + 1], shape)

    def row(array, at):
        return jnp.broadcast_to(array[at : at + 1, :], shape)

    for b in range(count):
        first = 8 * b
        inside = (lane >= first) & (lane < first + 8)
        columns = [column(blocks[b], first + k) for k in range(8)]
        entry = {(i, k): row(columns[k], i) for k in range(8) for i in range(k, 8)}
        cleared = jnp.where(inside, (lane - first == sublane).astype(jnp.float32), blocks[b])
        rows = [row(cleared, k) for k in range(8)]
        inverse = [None] * 8
        lower = {}
        for k in range(8):
            inverse[k] = pltpu.reciprocal(entry[k, k], approx=True)
            for i in range(k + 1, 8):
                lower[i, k] = entry[i, k] * inverse[k]
            for i in range(k + 1, 8):
                for j in range(k + 1, i + 1):
                    entry[i, j] = entry[i, j] - lower[i, k] * entry[j, k]
        for k in range(8):
            for m in range(k):
                rows[k] = rows[k] - lower[k, m] * rows[m]
        result = jnp.zeros(shape, jnp.float32)
        for k in range(8):
            result = jnp.where(sublane == k, rows[k] * lax.rsqrt(entry[k, k]), result)
        done.append(jnp.where(lane <= first + sublane, result, 0.0))
        if b + 1 == count:
            break
        for i in range(b + 1, count):
            target = blocks[i]
            factors = [column(target, first + k) for k in range(8)]
            target = jnp.where(inside, 0.0, target)
            for k in range(8):
                factor = factors[k] * inverse[k]
                for m in range(k + 1, 8):
                    factors[m] = factors[m] - factor * entry[m, k]
                target = target - factor * rows[k]
            blocks[i] = target
    return done


def finish_kernel(part_ref, gram_ref, near_ref, other_ref, across_ref, out_ref, inverse):
    columns = part_ref.shape[0]
    own = jnp.concatenate([part_ref[...], gram_ref[...]], axis=0)
    total = (own + across_ref[...]) + (near_ref[...] + other_ref[...])
    gram = unpack(total[columns:])
    for b, rows in enumerate(factor_rows([gram[8 * b : 8 * b + 8] for b in range(K // 8)])):
        inverse[pl.ds(8 * b, 8), :] = rows
    out_ref[...] = lax.dot_general(
        total[:columns], inverse[...], NT, precision=lax.Precision.HIGHEST, preferred_element_type=jnp.float32
    )


def finish_call(part, gram, got):
    vmem = pl.BlockSpec(memory_space=pltpu.VMEM)
    return pl.pallas_call(
        finish_kernel,
        out_shape=jax.ShapeDtypeStruct(part.shape, jnp.float32),
        in_specs=[vmem] * 5,
        out_specs=vmem,
        scratch_shapes=[pltpu.VMEM((K, K), jnp.float32)],
        compiler_params=pltpu.CompilerParams(vmem_limit_bytes=8 * 2**20),
        cost_estimate=pl.CostEstimate(flops=10**9, bytes_accessed=2**20, transcendentals=0),
        name="finish",
    )(part, gram, *got)


def swap_cores(array):
    return lax.ppermute(array, "rows", [(i, i ^ 1) for i in range(2 * SIDE**3)])


def swap_chips(array, axes, mask):
    pairs = []
    for chip in range(SIDE**3):
        for core, axis in enumerate(axes):
            target = list(place_of(chip))
            target[axis] ^= mask
            pairs.append((2 * chip + core, device(*target, core)))
    return lax.ppermute(array, "rows", pairs)


def body(slab, test_matrix):
    me = lax.axis_index("rows").astype(jnp.int32)
    place = jnp.stack([*place_of(me // 2), me % 2])
    slab = pltpu.with_memory_space_constraint(slab, pltpu.HBM)
    test_matrix = pltpu.with_memory_space_constraint(test_matrix, pltpu.HBM)
    gram, mine, other = sketch_call(place, slab, test_matrix)

    rows = SIDE**2 * 32
    mine, other = mine.reshape(SIDE, rows, K), other.reshape(SIDE, rows, K)
    got = swap_cores(jnp.concatenate([other[3], gram]))
    parts = [mine[i] + swap_cores(other[i]) for i in range(3)] + [mine[3] + got[:rows]]
    gram = gram + got[rows:]
    for number, axes in enumerate(AXES):
        stay, *leave = parts
        got = [swap_chips(jnp.concatenate([piece, gram]), axes, mask) for piece, mask in zip(leave, MASKS)]
        if number + 1 == len(AXES):
            return finish_call(stay, gram, got).T
        part = (stay + got[2][:rows]) + (got[0][:rows] + got[1][:rows])
        gram = (gram + got[2][rows:]) + (got[0][rows:] + got[1][rows:])
        rows //= 4
        parts = [part[i * rows : (i + 1) * rows] for i in range(4)]


def solution(mesh):
    return jax.shard_map(
        body, mesh=mesh, in_specs=(P("rows", None), P()), out_specs=P(None, "rows"), check_vma=False
    )
```

```python
import jax
import jax.numpy as jnp
from jax import lax
from jax.experimental import pallas as pl
from jax.experimental.pallas import tpu as pltpu
from jax.sharding import PartitionSpec as P

SIDE = 4
K = 128
CHUNK = 256
AHEAD = 4
COLS = 512
NT = (((1,), (1,)), ((), ()))


def place_of(chip):
    return chip // SIDE**2, chip // SIDE % SIDE, chip % SIDE


def turn(target, here):
    apart = target ^ here
    return 2 * ((apart >> 1) ^ (apart & 1)) + (apart >> 1)


def device(y, z, x, core):
    return ((y * SIDE + z) * SIDE + x) * 2 + core


def lanes(rows):
    return lax.broadcasted_iota(jnp.int32, (rows, K), 1)


def pack(gram):
    third = jnp.where(lanes(32) < 96, gram[64:96], pltpu.roll(gram[:32], 96, 1))
    second = jnp.where(lanes(16) < 64, gram[32:48], pltpu.roll(gram[48:64], 64, 1))
    return jnp.concatenate([gram[96:], third, second], axis=0)


def unpack(packed):
    third, second = packed[32:64], packed[64:80]
    low = [pltpu.roll(third, 32, 1), second, pltpu.roll(second, 64, 1), third, packed[:32]]
    low = jnp.concatenate(low, axis=0)
    row = lax.broadcasted_iota(jnp.int32, (K, K), 0)
    return jnp.where(row // 32 >= lanes(K) // 32, low, low.T)


def sketch_kernel(place_ref, slab_ref, omega_ref, gram_ref, mine_ref, other_ref, slab_v, omega_v, beside, above, sems, omega_sem):
    rows, width = slab_v.shape
    chunks = rows // CHUNK

    def copy(i):
        at = pl.ds(i * CHUNK, CHUNK)
        return pltpu.make_async_copy(slab_ref.at[at, :], slab_v.at[at, :], sems.at[i])

    def split(value):
        high = value.astype(jnp.bfloat16)
        return high, (value - high.astype(jnp.float32)).astype(jnp.bfloat16)

    omega_copy = pltpu.make_async_copy(omega_ref, omega_v, omega_sem)
    omega_copy.start()
    copy(0).start()
    omega_copy.wait()
    for i in range(1, AHEAD):
        copy(i).start()
    def keep(i, sketch):
        at = pl.ds(i * CHUNK, CHUNK)
        beside[at, :K], beside[at, K:] = split(sketch)
        above[:K, at], above[K:, at] = split(sketch.T)

    last = None
    for i in range(chunks):
        copy(i).wait()
        if i + AHEAD < chunks:
            copy(i + AHEAD).start()
        block = slab_v[pl.ds(i * CHUNK, CHUNK), :]
        sketch = jnp.dot(block, omega_v[...], preferred_element_type=jnp.float32)
        if i > 0:
            keep(i - 1, last)
        last = sketch
    keep(chunks - 1, last)
    gram = jnp.dot(above[...], beside[...], preferred_element_type=jnp.float32)
    gram_ref[...] = pack((gram[K:, K:] + (gram[:K, K:] + gram[K:, :K])) + gram[:K, :K])

    y, z, x, core = (place_ref[i] for i in range(4))
    first = core == 0
    for n in range(width // COLS):
        both = jnp.dot(above[...], slab_v[:, pl.ds(n * COLS, COLS)], preferred_element_type=jnp.float32)
        tile = (both[K:, :] + both[:K, :]).T.reshape(COLS // 64, 2, 32, K)
        for chip in range(COLS // 64):
            to_y, to_z, to_x = place_of(n * (COLS // 64) + chip)
            even, odd = tile[chip, 0], tile[chip, 1]
            by_y, by_z, by_x = turn(to_y, y), turn(to_z, z), turn(to_x, x)
            even_at = by_x, SIDE * by_y + by_z
            odd_at = by_z, SIDE * by_x + by_y
            mine_at = [jnp.where(first, p, q) for p, q in zip(even_at, odd_at)]
            other_at = [jnp.where(first, q, p) for p, q in zip(even_at, odd_at)]
            mine_ref[mine_at[0], mine_at[1]] = jnp.where(first, even, odd)
            other_ref[other_at[0], other_at[1]] = jnp.where(first, odd, even)


def sketch_call(place, slab, omega):
    rows, width = slab.shape
    vmem = pl.BlockSpec(memory_space=pltpu.VMEM)
    hbm = pl.BlockSpec(memory_space=pltpu.HBM)
    half = jax.ShapeDtypeStruct((SIDE, SIDE * SIDE, 32, K), jnp.float32)
    return pl.pallas_call(
        sketch_kernel,
        out_shape=(jax.ShapeDtypeStruct((80, K), jnp.float32), half, half),
        in_specs=[pl.BlockSpec(memory_space=pltpu.SMEM), hbm, hbm],
        out_specs=(vmem,) * 3,
        scratch_shapes=[
            pltpu.VMEM((rows, width), slab.dtype),
            pltpu.VMEM(omega.shape, omega.dtype),
            pltpu.VMEM((rows, 2 * K), jnp.bfloat16),
            pltpu.VMEM((2 * K, rows), jnp.bfloat16),
            pltpu.SemaphoreType.DMA((rows // CHUNK,)),
            pltpu.SemaphoreType.DMA,
        ],
        compiler_params=pltpu.CompilerParams(vmem_limit_bytes=36 * 2**20),
        cost_estimate=pl.CostEstimate(
            flops=2 * rows * width * 3 * K, bytes_accessed=2 * rows * width, transcendentals=0
        ),
        name="sketch",
    )(place, slab, omega)


AXES = (2, 1), (0, 2), (1, 0)
MASKS = 3, 1, 2


def factor_rows(blocks):
    shape = (8, K)
    lane = lax.broadcasted_iota(jnp.int32, shape, 1)
    sublane = lax.broadcasted_iota(jnp.int32, shape, 0)
    blocks = list(blocks)
    count = len(blocks)
    done = []

    def column(array, at):
        return jnp.broadcast_to(array[:, at : at + 1], shape)

    def row(array, at):
        return jnp.broadcast_to(array[at : at + 1, :], shape)

    for b in range(count):
        first = 8 * b
        inside = (lane >= first) & (lane < first + 8)
        columns = [column(blocks[b], first + k) for k in range(8)]
        entry = {(i, k): row(columns[k], i) for k in range(8) for i in range(k, 8)}
        cleared = jnp.where(inside, (lane - first == sublane).astype(jnp.float32), blocks[b])
        rows = [row(cleared, k) for k in range(8)]
        inverse = [None] * 8
        lower = {}
        for k in range(8):
            inverse[k] = pltpu.reciprocal(entry[k, k], approx=True)
            for i in range(k + 1, 8):
                lower[i, k] = entry[i, k] * inverse[k]
            for i in range(k + 1, 8):
                for j in range(k + 1, i + 1):
                    entry[i, j] = entry[i, j] - lower[i, k] * entry[j, k]
        for k in range(8):
            for m in range(k):
                rows[k] = rows[k] - lower[k, m] * rows[m]
        result = jnp.zeros(shape, jnp.float32)
        for k in range(8):
            result = jnp.where(sublane == k, rows[k] * lax.rsqrt(entry[k, k]), result)
        done.append(jnp.where(lane <= first + sublane, result, 0.0))
        if b + 1 == count:
            break
        for i in range(b + 1, count):
            target = blocks[i]
            factors = [column(target, first + k) for k in range(8)]
            target = jnp.where(inside, 0.0, target)
            for k in range(8):
                factor = factors[k] * inverse[k]
                for m in range(k + 1, 8):
                    factors[m] = factors[m] - factor * entry[m, k]
                target = target - factor * rows[k]
            blocks[i] = target
    return done


def finish_kernel(part_ref, gram_ref, near_ref, other_ref, across_ref, out_ref, inverse):
    columns = part_ref.shape[0]
    own = jnp.concatenate([part_ref[...], gram_ref[...]], axis=0)
    total = (own + across_ref[...]) + (near_ref[...] + other_ref[...])
    gram = unpack(total[columns:])
    for b, rows in enumerate(factor_rows([gram[8 * b : 8 * b + 8] for b in range(K // 8)])):
        inverse[pl.ds(8 * b, 8), :] = rows
    out_ref[...] = lax.dot_general(
        total[:columns], inverse[...], NT, precision=lax.Precision.HIGHEST, preferred_element_type=jnp.float32
    )


def finish_call(part, gram, got):
    vmem = pl.BlockSpec(memory_space=pltpu.VMEM)
    return pl.pallas_call(
        finish_kernel,
        out_shape=jax.ShapeDtypeStruct(part.shape, jnp.float32),
        in_specs=[vmem] * 5,
        out_specs=vmem,
        scratch_shapes=[pltpu.VMEM((K, K), jnp.float32)],
        compiler_params=pltpu.CompilerParams(vmem_limit_bytes=8 * 2**20),
        cost_estimate=pl.CostEstimate(flops=10**9, bytes_accessed=2**20, transcendentals=0),
        name="finish",
    )(part, gram, *got)


def swap_cores(array):
    return lax.ppermute(array, "rows", [(i, i ^ 1) for i in range(2 * SIDE**3)])


def swap_chips(array, axes, mask):
    pairs = []
    for chip in range(SIDE**3):
        for core, axis in enumerate(axes):
            target = list(place_of(chip))
            target[axis] ^= mask
            pairs.append((2 * chip + core, device(*target, core)))
    return lax.ppermute(array, "rows", pairs)


def body(slab, test_matrix):
    me = lax.axis_index("rows").astype(jnp.int32)
    place = jnp.stack([*place_of(me // 2), me % 2])
    slab = pltpu.with_memory_space_constraint(slab, pltpu.HBM)
    test_matrix = pltpu.with_memory_space_constraint(test_matrix, pltpu.HBM)
    gram, mine, other = sketch_call(place, slab, test_matrix)

    rows = SIDE**2 * 32
    mine, other = mine.reshape(SIDE, rows, K), other.reshape(SIDE, rows, K)
    got = swap_cores(jnp.concatenate([other[3], gram]))
    parts = [mine[i] + swap_cores(other[i]) for i in range(3)] + [mine[3] + got[:rows]]
    gram = gram + got[rows:]
    for number, axes in enumerate(AXES):
        stay, *leave = parts
        got = [swap_chips(jnp.concatenate([piece, gram]), axes, mask) for piece, mask in zip(leave, MASKS)]
        if number + 1 == len(AXES):
            return finish_call(stay, gram, got).T
        part = (stay + got[2][:rows]) + (got[0][:rows] + got[1][:rows])
        gram = (gram + got[2][rows:]) + (got[0][rows:] + got[1][rows:])
        rows //= 4
        parts = [part[i * rows : (i + 1) * rows] for i in range(4)]


def solution(mesh):
    return jax.shard_map(
        body, mesh=mesh, in_specs=(P("rows", None), P()), out_specs=P(None, "rows"), check_vma=False
    )
```
